512 devices in a mesh: module: 4 (over y_lo), dp: 128 (over x, y_hi, z, core).
Axes of the slice: x: 4, y: 8 (y_hi: 2, y_lo: 4; y = y_hi * 4 + y_lo), z: 8, core: 2. Of those that a mesh axis runs over, the one named last changes fastest.
Arguments:
- weight: bfloat16 [4, 1024, 1024], P('module'), may hold values from -0.1875 to 0.1875
- replay_buffer: bfloat16 [4, 2, 16384, 1024], P('module', None, 'dp'), may hold values from -6 to 6
- slot_index: int32 [4, 2], P('module'), may hold values from 0 to 1
- stem_input: bfloat16 [2, 16384, 1024], P(None, 'dp'), may hold values from -6 to 6
- top_grad: bfloat16 [2, 16384, 1024], P(None, 'dp'), may hold values from -6 to 6
- late_grad: bfloat16 [4, 16384, 1024], P('module', 'dp'), may hold values from -6 to 6
Outputs:
- weight_grad: bfloat16 [4, 1024, 1024], P('module')
- handoff: bfloat16 [4, 16384, 1024], P('module', 'dp')
- returned_grad: bfloat16 [4, 16384, 1024], P('module', 'dp')
The draws below stay inside these ranges and needn't reach their ends.
All inputs are finite; a program needn't handle non-finite values.
Results may differ from the reference program's by a relative error of at most 0.007.
Values may be sent and summed in bfloat16 or wider, within the bound.
No kernel may reach another device: no remote copies, remote signals or barrier semaphores. Data moves between devices by JAX's collectives and lax.ppermute only.
A program may use at most 64 MiB of HBM per device.

```python
import jax
import jax.numpy as jnp
from jax import lax

D = 1024
STEPS = 2
SLOTS = 2
MODULES = 4
TOKENS = 16384
N_MODULE = 4


def set_ends(result, own_key, low, largest):
    place = [jax.random.randint(jax.random.fold_in(own_key, axis), (), 0, length) for axis, length in enumerate(result.shape)]
    widest = result.shape.index(max(result.shape))
    neighbour = place[:widest] + [(place[widest] + 1) % result.shape[widest]] + place[widest + 1:]
    return result.at[tuple(place)].set(low).at[tuple(neighbour)].set(largest)


def block_levels(rng, dims, shards, least, largest):
    factor_of, own = 1.0, jax.random.fold_in(rng, 6)
    for position, shards_of in shards:
        draws = jnp.exp(jax.random.uniform(jax.random.fold_in(own, position), (shards_of,), jnp.float32, least / len(shards), largest / len(shards)))
        factor_of = factor_of * jnp.repeat(draws, dims[position] // shards_of).reshape([-1 if axis == position else 1 for axis in range(len(dims))])
    return factor_of


def centred(own_key, shape, scale, limit, shards=(), dtype=jnp.bfloat16):
    factor_of = block_levels(own_key, shape, shards, -0.22, 0.18) if shards else 1.0
    entries = jax.random.normal(own_key, shape, jnp.float32) * scale * factor_of
    return jnp.minimum(jnp.maximum(entries, -limit), limit).astype(dtype)


def setup_inputs(seed: int = 0) -> dict:
    key_list = jax.random.split(jax.random.key(seed), 7)
    weight = centred(key_list[0], (MODULES, D, D), D ** -0.5, 0.1875, ((0, 4),))
    replay_buffer = centred(key_list[1], (MODULES, SLOTS, TOKENS, D), 1.0, 6.0, ((0, 4), (2, 128)))
    slot_index = set_ends(jax.random.randint(key_list[2], (MODULES, STEPS), 0, SLOTS), jax.random.fold_in(key_list[2], 1), 0, SLOTS - 1).astype(jnp.int32)
    stem_input = centred(key_list[3], (STEPS, TOKENS, D), 1.0, 6.0, ((1, 128),))
    top_grad = centred(key_list[4], (STEPS, TOKENS, D), 1.0, 6.0, ((1, 128),))
    late_grad = centred(key_list[5], (MODULES, TOKENS, D), 1.0, 6.0, ((0, 4), (1, 128)))
    return dict(weight=weight, replay_buffer=replay_buffer, slot_index=slot_index, stem_input=stem_input, top_grad=top_grad, late_grad=late_grad)


def normalize(rows):
    values = rows.astype(jnp.float32)
    centered = values - lax.optimization_barrier(jnp.mean(values, axis=-1, keepdims=True))
    inverse = lax.rsqrt(lax.optimization_barrier(jnp.mean(centered * centered, axis=-1, keepdims=True)) + 1e-06)
    return (centered * inverse, inverse)

def forward(rows, matrix):
    normed, inverse = normalize(rows)
    preact = jnp.dot(normed.astype(jnp.bfloat16), matrix, preferred_element_type=jnp.float32)
    return (rows.astype(jnp.float32) + jax.nn.gelu(preact)).astype(jnp.bfloat16)

def backward(rows, matrix, upstream):
    normed, inverse = normalize(rows)
    rounded = normed.astype(jnp.bfloat16)
    preact = jnp.dot(rounded, matrix, preferred_element_type=jnp.float32)
    unused, pullback = jax.vjp(jax.nn.gelu, preact)
    pre_grad = pullback(upstream.astype(jnp.float32))[0].astype(jnp.bfloat16)
    weight_part = lax.dot_general(rounded, pre_grad, (((0,), (0,)), ((), ())), preferred_element_type=jnp.float32)
    norm_grad = lax.dot_general(pre_grad, matrix, (((1,), (1,)), ((), ())), preferred_element_type=jnp.float32)
    centred_grad = norm_grad - lax.optimization_barrier(jnp.mean(norm_grad, axis=-1, keepdims=True))
    centred_grad = centred_grad - normed * lax.optimization_barrier(jnp.mean(norm_grad * normed, axis=-1, keepdims=True))
    input_grad = upstream.astype(jnp.float32) + inverse * centred_grad
    return (input_grad.astype(jnp.bfloat16), weight_part)

def reference(weight, replay_buffer, slot_index, stem_input, top_grad, late_grad):
    modules = N_MODULE
    fresh_prev = []
    grads_prev = []
    summed = [jnp.zeros((D, D), jnp.float32) for module_number in range(modules)]
    for step_number in range(STEPS):
        fresh_now = []
        grads_now = []
        for module_number in range(modules):
            replayed = lax.dynamic_index_in_dim(replay_buffer[module_number], slot_index[module_number, step_number].astype(jnp.int32), 0, keepdims=False)
            if module_number == 0:
                fresh_in = stem_input[step_number]
            elif step_number == 0:
                fresh_in = replayed
            else:
                fresh_in = fresh_prev[module_number - 1]
            fresh_now.append(forward(fresh_in, weight[module_number]))
            if module_number == modules - 1:
                delayed = top_grad[step_number]
            elif step_number == 0:
                delayed = late_grad[module_number]
            else:
                delayed = grads_prev[module_number + 1]
            input_grad, weight_part = backward(replayed, weight[module_number], delayed)
            grads_now.append(input_grad)
            summed[module_number] = summed[module_number] + weight_part
        fresh_prev = fresh_now
        grads_prev = grads_now
    grad_scale = float(STEPS * TOKENS) ** (-0.5)
    weight_grad = jnp.stack([(part * grad_scale).astype(jnp.bfloat16) for part in summed])
    return (weight_grad, jnp.stack(fresh_prev), jnp.stack(grads_prev))
```

```python
import jax
import jax.numpy as jnp
from jax import lax
from jax.sharding import Mesh, PartitionSpec as P


def from_behind(block, axis, distance):
    devices = range(lax.axis_size(axis))
    route = [(i - distance, i) for i in devices if i - distance in devices]
    return lax.ppermute(block, axis, route)


def normalize(rows):
    values = rows.astype(jnp.float32)
    centered = values - jnp.mean(values, axis=-1, keepdims=True)
    inverse = lax.rsqrt(jnp.mean(centered * centered, axis=-1, keepdims=True) + 1e-06)
    return (centered * inverse, inverse)


def forward(rows, matrix):
    normed, inverse = normalize(rows)
    preact = jnp.dot(normed.astype(jnp.bfloat16), matrix, preferred_element_type=jnp.float32)
    return (rows.astype(jnp.float32) + jax.nn.gelu(preact)).astype(jnp.bfloat16)


def backward(rows, matrix, upstream):
    normed, inverse = normalize(rows)
    rounded = normed.astype(jnp.bfloat16)
    preact = jnp.dot(rounded, matrix, preferred_element_type=jnp.float32)
    unused, pullback = jax.vjp(jax.nn.gelu, preact)
    pre_grad = pullback(upstream.astype(jnp.float32))[0].astype(jnp.bfloat16)
    weight_part = lax.dot_general(
        rounded, pre_grad, (((0,), (0,)), ((), ())), preferred_element_type=jnp.float32
    )
    norm_grad = lax.dot_general(
        pre_grad, matrix, (((1,), (1,)), ((), ())), preferred_element_type=jnp.float32
    )
    centred_grad = norm_grad - jnp.mean(norm_grad, axis=-1, keepdims=True)
    centred_grad = centred_grad - normed * jnp.mean(norm_grad * normed, axis=-1, keepdims=True)
    input_grad = upstream.astype(jnp.float32) + inverse * centred_grad
    return (input_grad.astype(jnp.bfloat16), weight_part)


DP = ("x", "y_hi", "z", "core")
PLANE = ("x", "z")


def exchange(block, axes):
    return lax.all_to_all(block, axes, 0, 0, tiled=True)


def replica_sum(part, scale):
    rows, columns = part.shape
    cores, plane, halves = (lax.axis_size(axes) for axes in ("core", PLANE, "y_hi"))
    pair = exchange(part.astype(jnp.bfloat16), "core").reshape(cores, rows // cores, columns)
    chip = jnp.sum(pair.astype(jnp.float32), axis=0).astype(jnp.bfloat16)
    piece = rows // cores // plane
    spread = exchange(chip, PLANE).reshape(plane, piece, columns)
    own = jnp.sum(spread.astype(jnp.float32), axis=0)
    other = lax.ppermute(own, "y_hi", [(i, (i + 1) % halves) for i in range(halves)])
    total = ((own + other) * scale).astype(jnp.bfloat16)
    sent = jnp.broadcast_to(total[None], (plane, piece, columns)).reshape(plane * piece, columns)
    half = exchange(sent, PLANE)
    sent = jnp.broadcast_to(half[None], (cores, rows // cores, columns)).reshape(rows, columns)
    return exchange(sent, "core")


def per_device(weight, replay_buffer, slot_index, stem_input, top_grad, late_grad):
    matrix = weight[0]
    stored = replay_buffer[0]
    slot_rows = slot_index[0]
    module_number = lax.axis_index("module")
    module_count = lax.axis_size("module")
    is_first = module_number == 0
    is_last = module_number == module_count - 1
    returning = late_grad[0]
    step_count = stem_input.shape[0]
    summed = jnp.zeros(matrix.shape, jnp.float32)
    arriving = lax.dynamic_index_in_dim(stored, slot_rows[0], 0, keepdims=False)
    fresh_out = arriving
    sent_back = returning
    for step_number in range(step_count):
        replayed = lax.dynamic_index_in_dim(stored, slot_rows[step_number], 0, keepdims=False)
        fresh_in = jnp.where(is_first, stem_input[step_number], arriving)
        fresh_out = forward(fresh_in, matrix)
        delayed = jnp.where(is_last, top_grad[step_number], returning)
        sent_back, weight_part = backward(replayed, matrix, delayed)
        summed = summed + weight_part
        if step_number + 1 < step_count:
            arriving = from_behind(fresh_out, "module", 1)
            returning = from_behind(sent_back, "module", -1)
    replicas = lax.axis_size(DP)
    grad_scale = float(step_count * stem_input.shape[1] * replicas) ** (-0.5)
    weight_grad = replica_sum(summed, grad_scale)
    return (weight_grad[None], fresh_out[None], sent_back[None])


def solution(mesh):
    modules, replicas = (mesh.shape[name] for name in ("module", "dp"))
    fine = Mesh(
        mesh.devices.reshape(modules, 4, 2, replicas // 16, 2), ("module", *DP)
    )
    placed = (
        P("module", None, None),
        P("module", None, DP, None),
        P("module", None),
        P(None, DP, None),
        P(None, DP, None),
        P("module", DP, None),
    )
    return jax.shard_map(
        per_device,
        mesh=fine,
        in_specs=placed,
        out_specs=(P("module", None, None), P("module", DP, None), P("module", DP, None)),
        check_vma=False,
    )
```

```python
import jax
import jax.numpy as jnp
from jax import lax
from jax.experimental import pallas as pl
from jax.experimental.pallas import tpu as pltpu
from jax.sharding import Mesh, PartitionSpec as P

DP = ("x", "y_hi", "z", "core")
REST = ("y_hi", "z")
F32, BF16 = jnp.float32, jnp.bfloat16
GELU_SCALE, GELU_CUBE = 0.7978845608028654, 0.044715


def normalize(rows):
    values = rows.astype(F32)
    centered = values - jnp.mean(values, axis=-1, keepdims=True)
    inverse = lax.rsqrt(jnp.mean(centered * centered, axis=-1, keepdims=True) + 1e-06)
    return centered * inverse, inverse


def gelu(value):
    bent = jnp.tanh(GELU_SCALE * (value + GELU_CUBE * value * value * value))
    return 0.5 * value * (1.0 + bent)


def gelu_slope(value):
    square = value * value
    bent = jnp.tanh(GELU_SCALE * value * (1.0 + GELU_CUBE * square))
    inner = GELU_SCALE * (1.0 + 3.0 * GELU_CUBE * square)
    return 0.5 * (1.0 + bent) + 0.5 * value * (1.0 - bent * bent) * inner


def matmul(left, right, dims):
    return lax.dot_general(left, right, ((dims[:1], dims[1:]), ((), ())), preferred_element_type=F32)


def input_gradient(pre_grad, matrix, upstream, normed, inverse):
    norm_grad = matmul(pre_grad, matrix, (1, 1))
    inner = norm_grad - jnp.mean(norm_grad, axis=-1, keepdims=True)
    inner = inner - normed * jnp.mean(norm_grad * normed, axis=-1, keepdims=True)
    return (upstream.astype(F32) + inverse * inner).astype(BF16)


def call(kernel, in_specs, out_specs, outs, flops, scratch=()):
    return pl.pallas_call(
        kernel,
        out_shape=[jax.ShapeDtypeStruct(shape, dtype) for shape, dtype in outs],
        grid_spec=pltpu.PrefetchScalarGridSpec(
            num_scalar_prefetch=0,
            grid=(1,),
            in_specs=in_specs,
            out_specs=out_specs,
            scratch_shapes=list(scratch),
        ),
        compiler_params=pltpu.CompilerParams(vmem_limit_bytes=16 << 20),
        cost_estimate=pl.CostEstimate(flops=flops, bytes_accessed=2 << 20, transcendentals=0),
    )


IN_PLACE = pl.BlockSpec(memory_space=pl.ANY)
TICKET = (8, 128)


def in_hbm(*arrays):
    return [pltpu.with_memory_space_constraint(array, pltpu.HBM) for array in arrays]


def whole(shape):
    return pl.BlockSpec(shape, lambda _: (0,) * len(shape))


def wholes(*shapes):
    return [whole(shape) for shape in shapes]


def of_step(step, rows):
    return pl.BlockSpec((1, *rows), lambda _: (step, 0, 0))


def halves(block):
    half = block.shape[1] // 2
    near, far = block[:, :half], block[:, half:]
    left = lax.axis_index("core") == 0
    return jnp.where(left, near, far), jnp.where(left, far, near)


def on_last_module():
    return lax.axis_index("module") == lax.axis_size("module") - 1


def first_backward(
    slots, replay, matrix, late, top, sent, rounded, pre_grad, rows0, rows1,
    slot_at, stored, weights, late_rows, top_rows, done,
):
    pairs = (
        (slots, slot_at),
        (replay.at[0], stored),
        (late.at[0], late_rows),
        (top.at[0], top_rows),
        (matrix.at[0], weights),
    )
    copies = [
        pltpu.make_async_copy(source, target, done.at[number])
        for number, (source, target) in enumerate(pairs)
    ]
    for copy in copies:
        copy.start()
    for copy in copies[:2]:
        copy.wait()
    rows0[...] = stored[slot_at[0, 0]]
    rows1[...] = stored[slot_at[0, 1]]
    normed, inverse = normalize(rows0[...])
    rounded[...] = normed.astype(BF16)
    for copy in copies[2:]:
        copy.wait()
    upstream = jnp.where(on_last_module(), top_rows[...], late_rows[...])
    preact = matmul(rounded[...], weights[...], (1, 0))
    pre_grad[...] = (upstream.astype(F32) * gelu_slope(preact)).astype(BF16)
    sent[...] = input_gradient(pre_grad[...], weights[...], upstream, normed, inverse)


def second_slope(rows1, rounded0, pre_first, matrix, after, slope, packed, kept):
    count, half = kept.shape
    normed, _ = normalize(rows1[...])
    rounded = normed.astype(BF16)
    packed[:count] = rounded0[...]
    packed[count : 2 * count] = rounded
    kept[...], away = halves(pre_first[...])
    packed[2 * count :, :half] = away[: count // 2]
    packed[2 * count :, half:] = away[count // 2 :]
    slope[...] = gelu_slope(matmul(rounded, matrix[0], (1, 0)))


def second_grads(slope, returning, top, delayed, pre_grad, kept, given):
    upstream = jnp.where(on_last_module(), top[0], returning[...])
    pre = (upstream.astype(F32) * slope[...]).astype(BF16)
    delayed[...] = upstream
    pre_grad[...] = pre
    kept[...], given[...] = halves(pre)


def weight_half(packed, kept0, kept1, pair, pair1, after, part):
    count, half = kept0.shape
    middle = count // 2
    total = matmul(packed[:count], kept0[...], (0, 0))
    total += matmul(packed[count : 2 * count], kept1[...], (0, 0))
    total += matmul(pair[:middle], pair[2 * count :, :half], (0, 0))
    total += matmul(pair[middle:count], pair[2 * count :, half:], (0, 0))
    total += matmul(pair[count : 2 * count], pair1[...], (0, 0))
    part[...] = total.astype(BF16)


def returned(rows1, pre_grad, matrix, delayed, after, result, ticket):
    normed, inverse = normalize(rows1[...])
    result[0] = input_gradient(pre_grad[...], matrix[0], delayed[...], normed, inverse)
    ticket[...] = jnp.zeros(TICKET, F32)


def fresh(rows, matrix):
    normed, _ = normalize(rows)
    preact = matmul(normed.astype(BF16), matrix, (1, 0))
    return (rows.astype(F32) + gelu(preact)).astype(BF16)


def fresh_first(stem, rows0, matrix, result):
    rows = jnp.where(lax.axis_index("module") == 0, stem[0], rows0[...])
    result[...] = fresh(rows, matrix[0])


def fresh_second(stem, arriving, matrix, after, result, ticket):
    rows = jnp.where(lax.axis_index("module") == 0, stem[0], arriving[...])
    result[0] = fresh(rows, matrix[0])
    ticket[...] = jnp.zeros(TICKET, F32)


def joined(own, other, ticket0, ticket1, result, done):
    half = own.shape[1]
    here = lax.axis_index("core")
    copies = [
        pltpu.make_async_copy(
            block, result.at[0, :, pl.ds(pl.multiple_of(core * half, half), half)], done.at[number]
        )
        for number, (block, core) in enumerate(((own, here), (other, 1 - here)))
    ]
    for copy in copies:
        copy.start()
    for copy in copies:
        copy.wait()


def shift(block, axis, distance):
    devices = range(lax.axis_size(axis))
    route = [(i - distance, i) for i in devices if i - distance in devices]
    return lax.ppermute(block, axis, route)


def swap(block, axis):
    return lax.ppermute(block, axis, [(0, 1), (1, 0)])


def exchange(block, axes):
    return lax.all_to_all(block, axes, 0, 0, tiled=True)


def per_device(weight, replay_buffer, slot_index, stem_input, top_grad, late_grad):
    steps, count, width = stem_input.shape
    half = width // 2
    rows, columns, packing = (count, width), (count, half), (2 * count + count // 2, width)
    matrix, one = (1, width, width), 2 * count * width * width

    sent, rounded0, pre_first, rows0, rows1 = call(
        first_backward,
        [IN_PLACE] * 5,
        wholes(*[rows] * 5),
        [(rows, BF16)] * 5,
        2 * one,
        scratch=[
            pltpu.SMEM(slot_index.shape, jnp.int32),
            pltpu.VMEM(replay_buffer.shape[1:], BF16),
            pltpu.VMEM((width, width), BF16),
            pltpu.VMEM(rows, BF16),
            pltpu.VMEM(rows, BF16),
            pltpu.SemaphoreType.DMA((5,)),
        ],
    )(*in_hbm(slot_index, replay_buffer, weight, late_grad, top_grad))
    returning = shift(sent, "module", -1)
    (first_out,) = call(
        fresh_first,
        [of_step(0, rows), *wholes(rows, matrix)],
        wholes(rows),
        [(rows, BF16)],
        one,
    )(stem_input, rows0, weight)
    arriving = shift(first_out, "module", 1)
    slope, packed, kept0 = call(
        second_slope,
        [*wholes(rows, rows, rows, matrix), IN_PLACE],
        wholes(rows, packing, columns),
        [(rows, F32), (packing, BF16), (columns, BF16)],
        one,
    )(rows1, rounded0, pre_first, weight, first_out)
    pair = swap(packed, "core")
    delayed, pre_second, kept1, given1 = call(
        second_grads,
        [*wholes(rows, rows), of_step(1, rows)],
        wholes(rows, rows, columns, columns),
        [(rows, BF16), (rows, BF16), (columns, BF16), (columns, BF16)],
        count * width,
    )(slope, returning, top_grad)
    (part,) = call(
        weight_half,
        [*wholes(packing, columns, columns, packing, columns), IN_PLACE],
        wholes((width, half)),
        [((width, half), BF16)],
        2 * one,
    )(packed, kept0, kept1, pair, swap(given1, "core"), arriving)

    outer, inner = lax.axis_size("x"), lax.axis_size(REST)
    block, piece = width // outer, width // outer // inner
    spread = exchange(part, "x").reshape(outer, block, half)
    spread = exchange(jnp.sum(spread.astype(F32), axis=0).astype(BF16), REST)
    spread = spread.reshape(inner, piece, half).astype(F32)
    grad_scale = float(steps * count * lax.axis_size(DP)) ** (-0.5)
    total = (jnp.sum(spread, axis=0) * grad_scale).astype(BF16)
    total = jnp.broadcast_to(total[None], (inner, piece, half)).reshape(block, half)
    total = exchange(total, REST)
    total = jnp.broadcast_to(total[None], (outer, block, half)).reshape(width, half)
    total = exchange(total, "x")
    other = swap(total, "core")

    sent_back, ticket0 = call(
        returned,
        [*wholes(rows, rows, matrix, rows), IN_PLACE],
        wholes((1, *rows), TICKET),
        [((1, *rows), BF16), (TICKET, F32)],
        one,
    )(rows1, pre_second, weight, delayed, total)
    handoff, ticket1 = call(
        fresh_second,
        [of_step(1, rows), *wholes(rows, matrix), IN_PLACE],
        wholes((1, *rows), TICKET),
        [((1, *rows), BF16), (TICKET, F32)],
        one,
    )(stem_input, arriving, weight, total)
    (weight_grad,) = call(
        joined,
        [IN_PLACE] * 4,
        [IN_PLACE],
        [(matrix, BF16)],
        count * width,
        scratch=[pltpu.SemaphoreType.DMA((2,))],
    )(total, other, ticket0, ticket1)
    return weight_grad, handoff, sent_back


def solution(mesh):
    modules, replicas = (mesh.shape[name] for name in ("module", "dp"))
    fine = Mesh(mesh.devices.reshape(modules, 4, 2, replicas // 16, 2), ("module", *DP))
    placed = (
        P("module", None, None),
        P("module", None, DP, None),
        P("module", None),
        P(None, DP, None),
        P(None, DP, None),
        P("module", DP, None),
    )
    return jax.shard_map(
        per_device,
        mesh=fine,
        in_specs=placed,
        out_specs=(P("module", None, None), P("module", DP, None), P("module", DP, None)),
        check_vma=False,
    )
```

```python
import jax
import jax.numpy as jnp
from jax import lax
from jax.experimental import pallas as pl
from jax.experimental.pallas import tpu as pltpu
from jax.sharding import Mesh, PartitionSpec as P

DP = ("x", "y_hi", "z", "core")
REST = ("y_hi", "z")
F32, BF16 = jnp.float32, jnp.bfloat16
GELU_SCALE, GELU_CUBE = 0.7978845608028654, 0.044715


def normalize(rows):
    values = rows.astype(F32)
    centered = values - jnp.mean(values, axis=-1, keepdims=True)
    inverse = lax.rsqrt(jnp.mean(centered * centered, axis=-1, keepdims=True) + 1e-06)
    return centered * inverse, inverse


def gelu(value):
    bent = jnp.tanh(GELU_SCALE * (value + GELU_CUBE * value * value * value))
    return 0.5 * value * (1.0 + bent)


def gelu_slope(value):
    square = value * value
    bent = jnp.tanh(GELU_SCALE * value * (1.0 + GELU_CUBE * square))
    inner = GELU_SCALE * (1.0 + 3.0 * GELU_CUBE * square)
    return 0.5 * (1.0 + bent) + 0.5 * value * (1.0 - bent * bent) * inner


def matmul(left, right, dims):
    return lax.dot_general(left, right, ((dims[:1], dims[1:]), ((), ())), preferred_element_type=F32)


def input_gradient(pre_grad, matrix, upstream, normed, inverse):
    norm_grad = matmul(pre_grad, matrix, (1, 1))
    inner = norm_grad - jnp.mean(norm_grad, axis=-1, keepdims=True)
    inner = inner - normed * jnp.mean(norm_grad * normed, axis=-1, keepdims=True)
    return (upstream.astype(F32) + inverse * inner).astype(BF16)


def call(kernel, in_specs, out_specs, outs, flops, scratch=()):
    return pl.pallas_call(
        kernel,
        out_shape=[jax.ShapeDtypeStruct(shape, dtype) for shape, dtype in outs],
        grid_spec=pltpu.PrefetchScalarGridSpec(
            num_scalar_prefetch=0,
            grid=(1,),
            in_specs=in_specs,
            out_specs=out_specs,
            scratch_shapes=list(scratch),
        ),
        compiler_params=pltpu.CompilerParams(vmem_limit_bytes=16 << 20),
        cost_estimate=pl.CostEstimate(flops=flops, bytes_accessed=2 << 20, transcendentals=0),
    )


IN_PLACE = pl.BlockSpec(memory_space=pl.ANY)
TICKET = (8, 128)


def in_hbm(*arrays):
    return [pltpu.with_memory_space_constraint(array, pltpu.HBM) for array in arrays]


def whole(shape):
    return pl.BlockSpec(shape, lambda _: (0,) * len(shape))


def wholes(*shapes):
    return [whole(shape) for shape in shapes]


def of_step(step, rows):
    return pl.BlockSpec((1, *rows), lambda _: (step, 0, 0))


def halves(block):
    half = block.shape[1] // 2
    near, far = block[:, :half], block[:, half:]
    left = lax.axis_index("core") == 0
    return jnp.where(left, near, far), jnp.where(left, far, near)


def on_last_module():
    return lax.axis_index("module") == lax.axis_size("module") - 1


def first_backward(
    slots, replay, matrix, late, top, sent, rounded, pre_grad, rows0, rows1,
    slot_at, stored, weights, late_rows, top_rows, done,
):
    pairs = (
        (slots, slot_at),
        (replay.at[0], stored),
        (late.at[0], late_rows),
        (top.at[0], top_rows),
        (matrix.at[0], weights),
    )
    copies = [
        pltpu.make_async_copy(source, target, done.at[number])
        for number, (source, target) in enumerate(pairs)
    ]
    for copy in copies:
        copy.start()
    for copy in copies[:2]:
        copy.wait()
    rows0[...] = stored[slot_at[0, 0]]
    rows1[...] = stored[slot_at[0, 1]]
    normed, inverse = normalize(rows0[...])
    rounded[...] = normed.astype(BF16)
    for copy in copies[2:]:
        copy.wait()
    upstream = jnp.where(on_last_module(), top_rows[...], late_rows[...])
    preact = matmul(rounded[...], weights[...], (1, 0))
    pre_grad[...] = (upstream.astype(F32) * gelu_slope(preact)).astype(BF16)
    sent[...] = input_gradient(pre_grad[...], weights[...], upstream, normed, inverse)


def second_slope(rows1, matrix, rounded1, slope):
    normed, _ = normalize(rows1[...])
    rounded1[...] = normed.astype(BF16)
    slope[...] = gelu_slope(matmul(rounded1[...], matrix[0], (1, 0)))


def second_grads(
    rounded0, rounded1, pre_first, slope, returning, top, after, delayed, pre_grad, kept, packed
):
    count = rounded0.shape[0]
    half = kept.shape[1]
    upstream = jnp.where(on_last_module(), top[0], returning[...])
    pre = (upstream.astype(F32) * slope[...]).astype(BF16)
    delayed[...] = upstream
    pre_grad[...] = pre
    packed[:count] = rounded0[...]
    packed[count : 2 * count] = rounded1[...]
    kept[:count], packed[2 * count :, :half] = halves(pre_first[...])
    kept[count:], packed[2 * count :, half:] = halves(pre)


def weight_half(packed, kept, pair, ticket, part):
    count, half = kept.shape
    given = jnp.concatenate([pair[count:, :half], pair[count:, half:]], axis=0)
    total = matmul(packed[:count], kept[...], (0, 0))
    part[...] = (total + matmul(pair[:count], given, (0, 0))).astype(BF16)


def returned(rows1, pre_grad, matrix, delayed, result, ticket):
    normed, inverse = normalize(rows1[...])
    result[0] = input_gradient(pre_grad[...], matrix[0], delayed[...], normed, inverse)
    ticket[...] = jnp.zeros(TICKET, F32)


def fresh(rows, matrix):
    normed, _ = normalize(rows)
    preact = matmul(normed.astype(BF16), matrix, (1, 0))
    return (rows.astype(F32) + gelu(preact)).astype(BF16)


def fresh_first(stem, rows0, matrix, after, result):
    rows = jnp.where(lax.axis_index("module") == 0, stem[0], rows0[...])
    result[...] = fresh(rows, matrix[0])


def fresh_second(stem, arriving, matrix, after, result, ticket):
    rows = jnp.where(lax.axis_index("module") == 0, stem[0], arriving[...])
    result[0] = fresh(rows, matrix[0])
    ticket[...] = jnp.zeros(TICKET, F32)


def joined(own, other, ticket, result, done):
    half = own.shape[1]
    here = lax.axis_index("core")
    copies = [
        pltpu.make_async_copy(
            block, result.at[0, :, pl.ds(pl.multiple_of(core * half, half), half)], done.at[number]
        )
        for number, (block, core) in enumerate(((own, here), (other, 1 - here)))
    ]
    for copy in copies:
        copy.start()
    for copy in copies:
        copy.wait()


def shift(block, axis, distance):
    devices = range(lax.axis_size(axis))
    route = [(i - distance, i) for i in devices if i - distance in devices]
    return lax.ppermute(block, axis, route)


def swap(block, axis):
    return lax.ppermute(block, axis, [(0, 1), (1, 0)])


def exchange(block, axes):
    return lax.all_to_all(block, axes, 0, 0, tiled=True)


def per_device(weight, replay_buffer, slot_index, stem_input, top_grad, late_grad):
    steps, count, width = stem_input.shape
    half = width // 2
    rows, columns, packing = (count, width), (2 * count, half), (3 * count, width)
    matrix, one = (1, width, width), 2 * count * width * width

    sent, rounded0, pre_first, rows0, rows1 = call(
        first_backward,
        [IN_PLACE] * 5,
        wholes(*[rows] * 5),
        [(rows, BF16)] * 5,
        2 * one,
        scratch=[
            pltpu.SMEM(slot_index.shape, jnp.int32),
            pltpu.VMEM(replay_buffer.shape[1:], BF16),
            pltpu.VMEM((width, width), BF16),
            pltpu.VMEM(rows, BF16),
            pltpu.VMEM(rows, BF16),
            pltpu.SemaphoreType.DMA((5,)),
        ],
    )(*in_hbm(slot_index, replay_buffer, weight, late_grad, top_grad))
    returning = shift(sent, "module", -1)
    rounded1, slope = call(
        second_slope,
        wholes(rows, matrix),
        wholes(rows, rows),
        [(rows, BF16), (rows, F32)],
        one,
    )(rows1, weight)
    (first_out,) = call(
        fresh_first,
        [of_step(0, rows), *wholes(rows, matrix), IN_PLACE],
        wholes(rows),
        [(rows, BF16)],
        one,
    )(stem_input, rows0, weight, rounded1)
    arriving = shift(first_out, "module", 1)
    delayed, pre_second, kept, packed = call(
        second_grads,
        [*wholes(*[rows] * 5), of_step(1, rows), IN_PLACE],
        wholes(rows, rows, columns, packing),
        [(rows, BF16), (rows, BF16), (columns, BF16), (packing, BF16)],
        count * width,
    )(rounded0, rounded1, pre_first, slope, returning, top_grad, arriving)
    pair = swap(packed, "core")
    sent_back, ticket = call(
        returned,
        wholes(rows, rows, matrix, rows),
        wholes((1, *rows), TICKET),
        [((1, *rows), BF16), (TICKET, F32)],
        one,
    )(rows1, pre_second, weight, delayed)
    (part,) = call(
        weight_half,
        [*wholes(packing, columns, packing), IN_PLACE],
        wholes((width, half)),
        [((width, half), BF16)],
        2 * one,
    )(packed, kept, pair, ticket)

    outer, inner = lax.axis_size("x"), lax.axis_size(REST)
    block, piece = width // outer, width // outer // inner
    spread = exchange(part, "x").reshape(outer, block, half)
    spread = exchange(jnp.sum(spread.astype(F32), axis=0).astype(BF16), REST)
    spread = spread.reshape(inner, piece, half).astype(F32)
    grad_scale = float(steps * count * lax.axis_size(DP)) ** (-0.5)
    total = (jnp.sum(spread, axis=0) * grad_scale).astype(BF16)
    total = jnp.broadcast_to(total[None], (inner, piece, half)).reshape(block, half)
    total = exchange(total, REST)
    total = jnp.broadcast_to(total[None], (outer, block, half)).reshape(width, half)
    total = exchange(total, "x")
    other = swap(total, "core")

    handoff, ticket = call(
        fresh_second,
        [of_step(1, rows), *wholes(rows, matrix), IN_PLACE],
        wholes((1, *rows), TICKET),
        [((1, *rows), BF16), (TICKET, F32)],
        one,
    )(stem_input, arriving, *in_hbm(weight), total)
    (weight_grad,) = call(
        joined,
        [IN_PLACE] * 3,
        [IN_PLACE],
        [(matrix, BF16)],
        count * width,
        scratch=[pltpu.SemaphoreType.DMA((2,))],
    )(total, other, ticket)
    return weight_grad, handoff, sent_back


def solution(mesh):
    modules, replicas = (mesh.shape[name] for name in ("module", "dp"))
    fine = Mesh(mesh.devices.reshape(modules, 4, 2, replicas // 16, 2), ("module", *DP))
    placed = (
        P("module", None, None),
        P("module", None, DP, None),
        P("module", None),
        P(None, DP, None),
        P(None, DP, None),
        P("module", DP, None),
    )
    return jax.shard_map(
        per_device,
        mesh=fine,
        in_specs=placed,
        out_specs=(P("module", None, None), P("module", DP, None), P("module", DP, None)),
        check_vma=False,
    )
```

```python
import jax
import jax.numpy as jnp
from jax import lax
from jax.experimental import pallas as pl
from jax.experimental.pallas import tpu as pltpu
from jax.sharding import Mesh, PartitionSpec as P

DP = ("x", "y_hi", "z", "core")
REST = ("y_hi", "z")
F32, BF16 = jnp.float32, jnp.bfloat16
GELU_SCALE, GELU_CUBE = 0.7978845608028654, 0.044715


def normalize(rows):
    values = rows.astype(F32)
    centered = values - jnp.mean(values, axis=-1, keepdims=True)
    inverse = lax.rsqrt(jnp.mean(centered * centered, axis=-1, keepdims=True) + 1e-06)
    return centered * inverse, inverse


def gelu(value):
    bent = jnp.tanh(GELU_SCALE * (value + GELU_CUBE * value * value * value))
    return 0.5 * value * (1.0 + bent)


def gelu_slope(value):
    square = value * value
    bent = jnp.tanh(GELU_SCALE * value * (1.0 + GELU_CUBE * square))
    inner = GELU_SCALE * (1.0 + 3.0 * GELU_CUBE * square)
    return 0.5 * (1.0 + bent) + 0.5 * value * (1.0 - bent * bent) * inner


def matmul(left, right, dims):
    return lax.dot_general(left, right, ((dims[:1], dims[1:]), ((), ())), preferred_element_type=F32)


def input_gradient(pre_grad, matrix, upstream, normed, inverse):
    norm_grad = matmul(pre_grad, matrix, (1, 1))
    inner = norm_grad - jnp.mean(norm_grad, axis=-1, keepdims=True)
    inner = inner - normed * jnp.mean(norm_grad * normed, axis=-1, keepdims=True)
    return (upstream.astype(F32) + inverse * inner).astype(BF16)


def call(kernel, in_specs, out_specs, outs, flops, scratch=()):
    return pl.pallas_call(
        kernel,
        out_shape=[jax.ShapeDtypeStruct(shape, dtype) for shape, dtype in outs],
        grid_spec=pltpu.PrefetchScalarGridSpec(
            num_scalar_prefetch=0,
            grid=(1,),
            in_specs=in_specs,
            out_specs=out_specs,
            scratch_shapes=list(scratch),
        ),
        compiler_params=pltpu.CompilerParams(vmem_limit_bytes=16 << 20),
        cost_estimate=pl.CostEstimate(flops=flops, bytes_accessed=flops // 64, transcendentals=0),
    )


IN_PLACE = pl.BlockSpec(memory_space=pl.ANY)
TICKET = (8, 128)


def in_hbm(*arrays):
    return [pltpu.with_memory_space_constraint(array, pltpu.HBM) for array in arrays]


def whole(shape):
    return pl.BlockSpec(shape, lambda _: (0,) * len(shape))


def wholes(*shapes):
    return [whole(shape) for shape in shapes]


def of_step(step, rows):
    return pl.BlockSpec((1, *rows), lambda _: (step, 0, 0))


def halves(block):
    half = block.shape[1] // 2
    near, far = block[:, :half], block[:, half:]
    left = lax.axis_index("core") == 0
    return jnp.where(left, near, far), jnp.where(left, far, near)


def on_last_module():
    return lax.axis_index("module") == lax.axis_size("module") - 1


def first_backward(
    slots, replay, matrix, late, top, sent, rounded, pre_grad, rows0, rows1,
    slot_at, stored, weights, late_rows, top_rows, done,
):
    pairs = (
        (slots, slot_at),
        (replay.at[0], stored),
        (late.at[0], late_rows),
        (top.at[0], top_rows),
        (matrix.at[0], weights),
    )
    copies = [
        pltpu.make_async_copy(source, target, done.at[number])
        for number, (source, target) in enumerate(pairs)
    ]
    for copy in copies:
        copy.start()
    for copy in copies[:2]:
        copy.wait()
    rows0[...] = stored[slot_at[0, 0]]
    rows1[...] = stored[slot_at[0, 1]]
    normed, inverse = normalize(rows0[...])
    rounded[...] = normed.astype(BF16)
    for copy in copies[2:]:
        copy.wait()
    upstream = jnp.where(on_last_module(), top_rows[...], late_rows[...])
    preact = matmul(rounded[...], weights[...], (1, 0))
    pre_grad[...] = (upstream.astype(F32) * gelu_slope(preact)).astype(BF16)
    sent[...] = input_gradient(pre_grad[...], weights[...], upstream, normed, inverse)


def second_slope(rows1, matrix, rounded1, slope):
    normed, _ = normalize(rows1[...])
    rounded1[...] = normed.astype(BF16)
    slope[...] = gelu_slope(matmul(rounded1[...], matrix[0], (1, 0)))


def second_grads(
    rounded0, rounded1, pre_first, slope, returning, top, delayed, pre_grad, kept, packed
):
    count = rounded0.shape[0]
    half = kept.shape[1]
    upstream = jnp.where(on_last_module(), top[0], returning[...])
    pre = (upstream.astype(F32) * slope[...]).astype(BF16)
    delayed[...] = upstream
    pre_grad[...] = pre
    packed[:count] = rounded0[...]
    packed[count : 2 * count] = rounded1[...]
    kept[:count], packed[2 * count :, :half] = halves(pre_first[...])
    kept[count:], packed[2 * count :, half:] = halves(pre)


def weight_half(packed, kept, pair, ticket, part):
    count, half = kept.shape
    given = jnp.concatenate([pair[count:, :half], pair[count:, half:]], axis=0)
    total = matmul(packed[:count], kept[...], (0, 0))
    part[...] = (total + matmul(pair[:count], given, (0, 0))).astype(BF16)


def marker(ticket, after, result):
    result[...] = ticket[...]


def returned(rows1, pre_grad, matrix, delayed, result, ticket):
    normed, inverse = normalize(rows1[...])
    result[0] = input_gradient(pre_grad[...], matrix[0], delayed[...], normed, inverse)
    ticket[...] = jnp.zeros(TICKET, F32)


def fresh(rows, matrix):
    normed, _ = normalize(rows)
    preact = matmul(normed.astype(BF16), matrix, (1, 0))
    return (rows.astype(F32) + gelu(preact)).astype(BF16)


def fresh_first(stem, rows0, matrix, after, result):
    rows = jnp.where(lax.axis_index("module") == 0, stem[0], rows0[...])
    result[...] = fresh(rows, matrix[0])


def fresh_second(stem, arriving, matrix, after, result, ticket):
    rows = jnp.where(lax.axis_index("module") == 0, stem[0], arriving[...])
    result[0] = fresh(rows, matrix[0])
    ticket[...] = jnp.zeros(TICKET, F32)


def joined(own, other, ticket, result, done):
    half = own.shape[1]
    here = lax.axis_index("core")
    copies = [
        pltpu.make_async_copy(
            block, result.at[0, :, pl.ds(pl.multiple_of(core * half, half), half)], done.at[number]
        )
        for number, (block, core) in enumerate(((own, here), (other, 1 - here)))
    ]
    for copy in copies:
        copy.start()
    for copy in copies:
        copy.wait()


def shift(block, axis, distance):
    devices = range(lax.axis_size(axis))
    route = [(i - distance, i) for i in devices if i - distance in devices]
    return lax.ppermute(block, axis, route)


def swap(block, axis):
    return lax.ppermute(block, axis, [(0, 1), (1, 0)])


def exchange(block, axes):
    return lax.all_to_all(block, axes, 0, 0, tiled=True)


def per_device(weight, replay_buffer, slot_index, stem_input, top_grad, late_grad):
    steps, count, width = stem_input.shape
    half = width // 2
    rows, columns, packing = (count, width), (2 * count, half), (3 * count, width)
    matrix, one = (1, width, width), 2 * count * width * width

    sent, rounded0, pre_first, rows0, rows1 = call(
        first_backward,
        [IN_PLACE] * 5,
        wholes(*[rows] * 5),
        [(rows, BF16)] * 5,
        2 * one,
        scratch=[
            pltpu.SMEM(slot_index.shape, jnp.int32),
            pltpu.VMEM(replay_buffer.shape[1:], BF16),
            pltpu.VMEM((width, width), BF16),
            pltpu.VMEM(rows, BF16),
            pltpu.VMEM(rows, BF16),
            pltpu.SemaphoreType.DMA((5,)),
        ],
    )(*in_hbm(slot_index, replay_buffer, weight, late_grad, top_grad))
    returning = shift(sent, "module", -1)
    rounded1, slope = call(
        second_slope,
        wholes(rows, matrix),
        wholes(rows, rows),
        [(rows, BF16), (rows, F32)],
        one,
    )(rows1, weight)
    (first_out,) = call(
        fresh_first,
        [of_step(0, rows), *wholes(rows, matrix), IN_PLACE],
        wholes(rows),
        [(rows, BF16)],
        one,
    )(stem_input, rows0, weight, rounded1)
    arriving = shift(first_out, "module", 1)
    delayed, pre_second, kept, packed = call(
        second_grads,
        [*wholes(*[rows] * 5), of_step(1, rows)],
        wholes(rows, rows, columns, packing),
        [(rows, BF16), (rows, BF16), (columns, BF16), (packing, BF16)],
        count * width,
    )(rounded0, rounded1, pre_first, slope, returning, top_grad)
    pair = swap(packed, "core")
    sent_back, ticket = call(
        returned,
        wholes(rows, rows, matrix, rows),
        wholes((1, *rows), TICKET),
        [((1, *rows), BF16), (TICKET, F32)],
        count,
    )(rows1, pre_second, weight, delayed)
    (ticket,) = call(
        marker, [whole(TICKET), IN_PLACE], wholes(TICKET), [(TICKET, F32)], 100000000000
    )(ticket, arriving)
    (part,) = call(
        weight_half,
        [*wholes(packing, columns, packing), IN_PLACE],
        wholes((width, half)),
        [((width, half), BF16)],
        2 * one,
    )(packed, kept, pair, ticket)

    outer, inner = lax.axis_size("x"), lax.axis_size(REST)
    block, piece = width // outer, width // outer // inner
    spread = exchange(part, "x").reshape(outer, block, half)
    spread = exchange(jnp.sum(spread.astype(F32), axis=0).astype(BF16), REST)
    spread = spread.reshape(inner, piece, half).astype(F32)
    grad_scale = float(steps * count * lax.axis_size(DP)) ** (-0.5)
    total = (jnp.sum(spread, axis=0) * grad_scale).astype(BF16)
    total = jnp.broadcast_to(total[None], (inner, piece, half)).reshape(block, half)
    total = exchange(total, REST)
    total = jnp.broadcast_to(total[None], (outer, block, half)).reshape(width, half)
    total = exchange(total, "x")
    other = swap(total, "core")

    handoff, ticket = call(
        fresh_second,
        [of_step(1, rows), *wholes(rows, matrix), IN_PLACE],
        wholes((1, *rows), TICKET),
        [((1, *rows), BF16), (TICKET, F32)],
        one,
    )(stem_input, arriving, *in_hbm(weight), total)
    (weight_grad,) = call(
        joined,
        [IN_PLACE] * 3,
        [IN_PLACE],
        [(matrix, BF16)],
        count * width,
        scratch=[pltpu.SemaphoreType.DMA((2,))],
    )(total, other, ticket)
    return weight_grad, handoff, sent_back


def solution(mesh):
    modules, replicas = (mesh.shape[name] for name in ("module", "dp"))
    fine = Mesh(mesh.devices.reshape(modules, 4, 2, replicas // 16, 2), ("module", *DP))
    placed = (
        P("module", None, None),
        P("module", None, DP, None),
        P("module", None),
        P(None, DP, None),
        P(None, DP, None),
        P("module", DP, None),
    )
    return jax.shard_map(
        per_device,
        mesh=fine,
        in_specs=placed,
        out_specs=(P("module", None, None), P("module", DP, None), P("module", DP, None)),
        check_vma=False,
    )
```

```python
import jax
import jax.numpy as jnp
from jax import lax
from jax.experimental import pallas as pl
from jax.experimental.pallas import tpu as pltpu
from jax.sharding import Mesh, PartitionSpec as P

DP = ("x", "y_hi", "z", "core")
REST = ("y_hi", "z")
F32, BF16 = jnp.float32, jnp.bfloat16
GELU_SCALE, GELU_CUBE = 0.7978845608028654, 0.044715


def normalize(rows):
    values = rows.astype(F32)
    centered = values - jnp.mean(values, axis=-1, keepdims=True)
    inverse = lax.rsqrt(jnp.mean(centered * centered, axis=-1, keepdims=True) + 1e-06)
    return centered * inverse, inverse


def gelu(value):
    bent = jnp.tanh(GELU_SCALE * (value + GELU_CUBE * value * value * value))
    return 0.5 * value * (1.0 + bent)


def gelu_slope(value):
    square = value * value
    bent = jnp.tanh(GELU_SCALE * value * (1.0 + GELU_CUBE * square))
    inner = GELU_SCALE * (1.0 + 3.0 * GELU_CUBE * square)
    return 0.5 * (1.0 + bent) + 0.5 * value * (1.0 - bent * bent) * inner


def matmul(left, right, dims):
    return lax.dot_general(left, right, ((dims[:1], dims[1:]), ((), ())), preferred_element_type=F32)


def input_gradient(pre_grad, matrix, upstream, normed, inverse):
    norm_grad = matmul(pre_grad, matrix, (1, 1))
    inner = norm_grad - jnp.mean(norm_grad, axis=-1, keepdims=True)
    inner = inner - normed * jnp.mean(norm_grad * normed, axis=-1, keepdims=True)
    return (upstream.astype(F32) + inverse * inner).astype(BF16)


def call(kernel, in_specs, out_specs, outs, flops, scratch=(), aliases=None):
    return pl.pallas_call(
        kernel,
        out_shape=[jax.ShapeDtypeStruct(shape, dtype) for shape, dtype in outs],
        grid_spec=pltpu.PrefetchScalarGridSpec(
            num_scalar_prefetch=0,
            grid=(1,),
            in_specs=in_specs,
            out_specs=out_specs,
            scratch_shapes=list(scratch),
        ),
        input_output_aliases=aliases or {},
        compiler_params=pltpu.CompilerParams(vmem_limit_bytes=16 << 20),
        cost_estimate=pl.CostEstimate(flops=flops, bytes_accessed=flops // 64, transcendentals=0),
    )


IN_PLACE = pl.BlockSpec(memory_space=pl.ANY)
TICKET = (8, 128)


def in_hbm(*arrays):
    return [pltpu.with_memory_space_constraint(array, pltpu.HBM) for array in arrays]


def whole(shape):
    return pl.BlockSpec(shape, lambda _: (0,) * len(shape))


def wholes(*shapes):
    return [whole(shape) for shape in shapes]


def of_step(step, rows):
    return pl.BlockSpec((1, *rows), lambda _: (step, 0, 0))


def halves(block):
    half = block.shape[1] // 2
    near, far = block[:, :half], block[:, half:]
    left = lax.axis_index("core") == 0
    return jnp.where(left, near, far), jnp.where(left, far, near)


def on_last_module():
    return lax.axis_index("module") == lax.axis_size("module") - 1


def first_backward(
    slots, replay, matrix, late, top, sent, rounded, pre_grad, rows0, rows1,
    slot_at, stored, weights, late_rows, top_rows, done,
):
    pairs = (
        (slots, slot_at),
        (replay.at[0], stored),
        (late.at[0], late_rows),
        (top.at[0], top_rows),
        (matrix.at[0], weights),
    )
    copies = [
        pltpu.make_async_copy(source, target, done.at[number])
        for number, (source, target) in enumerate(pairs)
    ]
    for copy in copies:
        copy.start()
    for copy in copies[:2]:
        copy.wait()
    rows0[...] = stored[slot_at[0, 0]]
    rows1[...] = stored[slot_at[0, 1]]
    normed, inverse = normalize(rows0[...])
    rounded[...] = normed.astype(BF16)
    for copy in copies[2:]:
        copy.wait()
    upstream = jnp.where(on_last_module(), top_rows[...], late_rows[...])
    preact = matmul(rounded[...], weights[...], (1, 0))
    pre_grad[...] = (upstream.astype(F32) * gelu_slope(preact)).astype(BF16)
    sent[...] = input_gradient(pre_grad[...], weights[...], upstream, normed, inverse)


def second_slope(rows1, matrix, rounded1, slope):
    normed, _ = normalize(rows1[...])
    rounded1[...] = normed.astype(BF16)
    slope[...] = gelu_slope(matmul(rounded1[...], matrix[0], (1, 0)))


def second_grads(
    rounded0, rounded1, pre_first, slope, returning, top, delayed, pre_grad, kept, packed
):
    count = rounded0.shape[0]
    half = kept.shape[1]
    upstream = jnp.where(on_last_module(), top[0], returning[...])
    pre = (upstream.astype(F32) * slope[...]).astype(BF16)
    delayed[...] = upstream
    pre_grad[...] = pre
    packed[:count] = rounded0[...]
    packed[count : 2 * count] = rounded1[...]
    kept[:count], packed[2 * count :, :half] = halves(pre_first[...])
    kept[count:], packed[2 * count :, half:] = halves(pre)


def weight_half(packed, kept, pair, ticket, part):
    count, half = kept.shape
    given = jnp.concatenate([pair[count:, :half], pair[count:, half:]], axis=0)
    total = matmul(packed[:count], kept[...], (0, 0))
    part[...] = (total + matmul(pair[:count], given, (0, 0))).astype(BF16)


def marker(ticket, after, result):
    result[...] = ticket[...]


def returned(rows1, pre_grad, matrix, delayed, result, ticket):
    normed, inverse = normalize(rows1[...])
    result[0] = input_gradient(pre_grad[...], matrix[0], delayed[...], normed, inverse)
    ticket[...] = jnp.zeros(TICKET, F32)


def fresh(rows, matrix):
    normed, _ = normalize(rows)
    preact = matmul(normed.astype(BF16), matrix, (1, 0))
    return (rows.astype(F32) + gelu(preact)).astype(BF16)


def fresh_first(stem, rows0, matrix, after, result):
    rows = jnp.where(lax.axis_index("module") == 0, stem[0], rows0[...])
    result[...] = fresh(rows, matrix[0])


def fresh_second(stem, arriving, matrix, own, handoff, result, done):
    copy = pltpu.make_async_copy(own, columns_of(result, own, 0), done.at[0])
    copy.start()
    rows = jnp.where(lax.axis_index("module") == 0, stem[0], arriving[...])
    handoff[0] = fresh(rows, matrix[0])
    copy.wait()


def block_sum(spread, result):
    result[...] = jnp.sum(spread[...].astype(F32), axis=0).astype(BF16)


def columns_of(result, block, core):
    half = block.shape[1]
    place = lax.rem(lax.axis_index("core") + core, 2)
    return result.at[0, :, pl.ds(pl.multiple_of(place * half, half), half)]


def joined(partial, other, result, done):
    copy = pltpu.make_async_copy(other, columns_of(result, other, 1), done.at[0])
    copy.start()
    copy.wait()


def shift(block, axis, distance):
    devices = range(lax.axis_size(axis))
    route = [(i - distance, i) for i in devices if i - distance in devices]
    return lax.ppermute(block, axis, route)


def swap(block, axis):
    return lax.ppermute(block, axis, [(0, 1), (1, 0)])


def exchange(block, axes):
    return lax.all_to_all(block, axes, 0, 0, tiled=True)


def per_device(weight, replay_buffer, slot_index, stem_input, top_grad, late_grad):
    steps, count, width = stem_input.shape
    half = width // 2
    rows, columns, packing = (count, width), (2 * count, half), (3 * count, width)
    matrix, one = (1, width, width), 2 * count * width * width

    sent, rounded0, pre_first, rows0, rows1 = call(
        first_backward,
        [IN_PLACE] * 5,
        wholes(*[rows] * 5),
        [(rows, BF16)] * 5,
        2 * one,
        scratch=[
            pltpu.SMEM(slot_index.shape, jnp.int32),
            pltpu.VMEM(replay_buffer.shape[1:], BF16),
            pltpu.VMEM((width, width), BF16),
            pltpu.VMEM(rows, BF16),
            pltpu.VMEM(rows, BF16),
            pltpu.SemaphoreType.DMA((5,)),
        ],
    )(*in_hbm(slot_index, replay_buffer, weight, late_grad, top_grad))
    returning = shift(sent, "module", -1)
    rounded1, slope = call(
        second_slope,
        wholes(rows, matrix),
        wholes(rows, rows),
        [(rows, BF16), (rows, F32)],
        one,
    )(rows1, weight)
    (first_out,) = call(
        fresh_first,
        [of_step(0, rows), *wholes(rows, matrix), IN_PLACE],
        wholes(rows),
        [(rows, BF16)],
        one,
    )(stem_input, rows0, weight, rounded1)
    arriving = shift(first_out, "module", 1)
    delayed, pre_second, kept, packed = call(
        second_grads,
        [*wholes(*[rows] * 5), of_step(1, rows)],
        wholes(rows, rows, columns, packing),
        [(rows, BF16), (rows, BF16), (columns, BF16), (packing, BF16)],
        count * width,
    )(rounded0, rounded1, pre_first, slope, returning, top_grad)
    pair = swap(packed, "core")
    sent_back, ticket = call(
        returned,
        wholes(rows, rows, matrix, rows),
        wholes((1, *rows), TICKET),
        [((1, *rows), BF16), (TICKET, F32)],
        count,
    )(rows1, pre_second, weight, delayed)
    (ticket,) = call(
        marker, [whole(TICKET), IN_PLACE], wholes(TICKET), [(TICKET, F32)], 100000000000
    )(ticket, arriving)
    (part,) = call(
        weight_half,
        [*wholes(packing, columns, packing), IN_PLACE],
        wholes((width, half)),
        [((width, half), BF16)],
        2 * one,
    )(packed, kept, pair, ticket)

    outer, inner = lax.axis_size("x"), lax.axis_size(REST)
    block, piece = width // outer, width // outer // inner
    spread = exchange(part, "x").reshape(outer, block, half)
    (spread,) = call(
        block_sum,
        wholes((outer, block, half)),
        wholes((block, half)),
        [((block, half), BF16)],
        count * width,
    )(spread)
    spread = exchange(spread, REST)
    spread = spread.reshape(inner, piece, half).astype(F32)
    grad_scale = float(steps * count * lax.axis_size(DP)) ** (-0.5)
    total = (jnp.sum(spread, axis=0) * grad_scale).astype(BF16)
    total = jnp.broadcast_to(total[None], (inner, piece, half)).reshape(block, half)
    total = exchange(total, REST)
    total = jnp.broadcast_to(total[None], (outer, block, half)).reshape(width, half)
    total = exchange(total, "x")
    other = swap(total, "core")

    handoff, partial = call(
        fresh_second,
        [of_step(1, rows), *wholes(rows, matrix), IN_PLACE],
        [whole((1, *rows)), IN_PLACE],
        [((1, *rows), BF16), (matrix, BF16)],
        one,
        scratch=[pltpu.SemaphoreType.DMA((1,))],
    )(*in_hbm(stem_input), arriving, weight, total)
    (weight_grad,) = call(
        joined,
        [IN_PLACE] * 2,
        [IN_PLACE],
        [(matrix, BF16)],
        count * width,
        scratch=[pltpu.SemaphoreType.DMA((1,))],
        aliases={0: 0},
    )(partial, other)
    return weight_grad, handoff, sent_back


def solution(mesh):
    modules, replicas = (mesh.shape[name] for name in ("module", "dp"))
    fine = Mesh(mesh.devices.reshape(modules, 4, 2, replicas // 16, 2), ("module", *DP))
    placed = (
        P("module", None, None),
        P("module", None, DP, None),
        P("module", None),
        P(None, DP, None),
        P(None, DP, None),
        P("module", DP, None),
    )
    return jax.shard_map(
        per_device,
        mesh=fine,
        in_specs=placed,
        out_specs=(P("module", None, None), P("module", DP, None), P("module", DP, None)),
        check_vma=False,
    )
```

```python
import jax
import jax.numpy as jnp
from jax import lax
from jax.experimental import pallas as pl
from jax.experimental.pallas import tpu as pltpu
from jax.sharding import Mesh, PartitionSpec as P

DP = ("x", "y_hi", "z", "core")
REST = ("y_hi", "z")
F32, BF16 = jnp.float32, jnp.bfloat16
GELU_SCALE, GELU_CUBE = 0.7978845608028654, 0.044715


def normalize(rows):
    values = rows.astype(F32)
    centered = values - jnp.mean(values, axis=-1, keepdims=True)
    inverse = lax.rsqrt(jnp.mean(centered * centered, axis=-1, keepdims=True) + 1e-06)
    return centered * inverse, inverse


def gelu(value):
    bent = jnp.tanh(GELU_SCALE * (value + GELU_CUBE * value * value * value))
    return 0.5 * value * (1.0 + bent)


def gelu_slope(value):
    square = value * value
    bent = jnp.tanh(GELU_SCALE * value * (1.0 + GELU_CUBE * square))
    inner = GELU_SCALE * (1.0 + 3.0 * GELU_CUBE * square)
    return 0.5 * (1.0 + bent) + 0.5 * value * (1.0 - bent * bent) * inner


def matmul(left, right, dims):
    return lax.dot_general(left, right, ((dims[:1], dims[1:]), ((), ())), preferred_element_type=F32)


def input_gradient(pre_grad, matrix, upstream, normed, inverse):
    norm_grad = matmul(pre_grad, matrix, (1, 1))
    inner = norm_grad - jnp.mean(norm_grad, axis=-1, keepdims=True)
    inner = inner - normed * jnp.mean(norm_grad * normed, axis=-1, keepdims=True)
    return (upstream.astype(F32) + inverse * inner).astype(BF16)


def call(kernel, in_specs, out_specs, outs, flops, scratch=(), aliases=None):
    return pl.pallas_call(
        kernel,
        out_shape=[jax.ShapeDtypeStruct(shape, dtype) for shape, dtype in outs],
        grid_spec=pltpu.PrefetchScalarGridSpec(
            num_scalar_prefetch=0,
            grid=(1,),
            in_specs=in_specs,
            out_specs=out_specs,
            scratch_shapes=list(scratch),
        ),
        input_output_aliases=aliases or {},
        compiler_params=pltpu.CompilerParams(vmem_limit_bytes=16 << 20),
        cost_estimate=pl.CostEstimate(flops=flops, bytes_accessed=flops // 64, transcendentals=0),
    )


IN_PLACE = pl.BlockSpec(memory_space=pl.ANY)
TICKET = (8, 128)


def in_hbm(*arrays):
    return [pltpu.with_memory_space_constraint(array, pltpu.HBM) for array in arrays]


def whole(shape):
    return pl.BlockSpec(shape, lambda _: (0,) * len(shape))


def wholes(*shapes):
    return [whole(shape) for shape in shapes]


def of_step(step, rows):
    return pl.BlockSpec((1, *rows), lambda _: (step, 0, 0))


def halves(block):
    half = block.shape[1] // 2
    near, far = block[:, :half], block[:, half:]
    left = lax.axis_index("core") == 0
    return jnp.where(left, near, far), jnp.where(left, far, near)


def on_last_module():
    return lax.axis_index("module") == lax.axis_size("module") - 1


def first_backward(
    slots, replay, matrix, late, top, sent, rounded, pre_grad, rows0, rows1,
    slot_at, stored, weights, late_rows, top_rows, done,
):
    pairs = (
        (slots, slot_at),
        (replay.at[0], stored),
        (late.at[0], late_rows),
        (top.at[0], top_rows),
        (matrix.at[0], weights),
    )
    copies = [
        pltpu.make_async_copy(source, target, done.at[number])
        for number, (source, target) in enumerate(pairs)
    ]
    for copy in copies:
        copy.start()
    for copy in copies[:2]:
        copy.wait()
    rows0[...] = stored[slot_at[0, 0]]
    rows1[...] = stored[slot_at[0, 1]]
    normed, inverse = normalize(rows0[...])
    rounded[...] = normed.astype(BF16)
    for copy in copies[2:]:
        copy.wait()
    upstream = jnp.where(on_last_module(), top_rows[...], late_rows[...])
    preact = matmul(rounded[...], weights[...], (1, 0))
    pre_grad[...] = (upstream.astype(F32) * gelu_slope(preact)).astype(BF16)
    sent[...] = input_gradient(pre_grad[...], weights[...], upstream, normed, inverse)


def second_slope(rows1, matrix, rounded1, slope):
    normed, _ = normalize(rows1[...])
    rounded1[...] = normed.astype(BF16)
    slope[...] = gelu_slope(matmul(rounded1[...], matrix[0], (1, 0)))


def second_grads(
    rounded0, rounded1, pre_first, slope, returning, top, delayed, pre_grad, kept, packed
):
    count = rounded0.shape[0]
    half = kept.shape[1]
    upstream = jnp.where(on_last_module(), top[0], returning[...])
    pre = (upstream.astype(F32) * slope[...]).astype(BF16)
    delayed[...] = upstream
    pre_grad[...] = pre
    packed[:count] = rounded0[...]
    packed[count : 2 * count] = rounded1[...]
    kept[:count], packed[2 * count :, :half] = halves(pre_first[...])
    kept[count:], packed[2 * count :, half:] = halves(pre)


def weight_half(packed, kept, pair, ticket, part):
    count, half = kept.shape
    given = jnp.concatenate([pair[count:, :half], pair[count:, half:]], axis=0)
    total = matmul(packed[:count], kept[...], (0, 0))
    part[...] = (total + matmul(pair[:count], given, (0, 0))).astype(BF16)


def marker(ticket, after, result):
    result[...] = ticket[...]


def returned(rows1, pre_grad, matrix, delayed, result, ticket):
    normed, inverse = normalize(rows1[...])
    result[0] = input_gradient(pre_grad[...], matrix[0], delayed[...], normed, inverse)
    ticket[...] = jnp.zeros(TICKET, F32)


def fresh(rows, matrix):
    normed, _ = normalize(rows)
    preact = matmul(normed.astype(BF16), matrix, (1, 0))
    return (rows.astype(F32) + gelu(preact)).astype(BF16)


def fresh_first(stem, rows0, matrix, after, result):
    rows = jnp.where(lax.axis_index("module") == 0, stem[0], rows0[...])
    result[...] = fresh(rows, matrix[0])


def fresh_second(stem, arriving, matrix, own, handoff, result, done):
    copy = pltpu.make_async_copy(own, columns_of(result, own, 0), done.at[0])
    copy.start()
    rows = jnp.where(lax.axis_index("module") == 0, stem[0], arriving[...])
    handoff[0] = fresh(rows, matrix[0])
    copy.wait()


def block_sum(spread, result):
    result[...] = jnp.sum(spread[...].astype(F32), axis=0).astype(BF16)


def columns_of(result, block, core):
    half = block.shape[1]
    place = lax.rem(lax.axis_index("core") + core, 2)
    return result.at[0, :, pl.ds(pl.multiple_of(place * half, half), half)]


def joined(partial, other, result, done):
    copy = pltpu.make_async_copy(other, columns_of(result, other, 1), done.at[0])
    copy.start()
    copy.wait()


def shift(block, axis, distance):
    devices = range(lax.axis_size(axis))
    route = [(i - distance, i) for i in devices if i - distance in devices]
    return lax.ppermute(block, axis, route)


def swap(block, axis):
    return lax.ppermute(block, axis, [(0, 1), (1, 0)])


def exchange(block, axes):
    return lax.all_to_all(block, axes, 0, 0, tiled=True)


def per_device(weight, replay_buffer, slot_index, stem_input, top_grad, late_grad):
    steps, count, width = stem_input.shape
    half = width // 2
    rows, columns, packing = (count, width), (2 * count, half), (3 * count, width)
    matrix, one = (1, width, width), 2 * count * width * width

    sent, rounded0, pre_first, rows0, rows1 = call(
        first_backward,
        [IN_PLACE] * 5,
        wholes(*[rows] * 5),
        [(rows, BF16)] * 5,
        2 * one,
        scratch=[
            pltpu.SMEM(slot_index.shape, jnp.int32),
            pltpu.VMEM(replay_buffer.shape[1:], BF16),
            pltpu.VMEM((width, width), BF16),
            pltpu.VMEM(rows, BF16),
            pltpu.VMEM(rows, BF16),
            pltpu.SemaphoreType.DMA((5,)),
        ],
    )(*in_hbm(slot_index, replay_buffer, weight, late_grad, top_grad))
    returning = shift(sent, "module", -1)
    rounded1, slope = call(
        second_slope,
        wholes(rows, matrix),
        wholes(rows, rows),
        [(rows, BF16), (rows, F32)],
        one,
    )(rows1, weight)
    (first_out,) = call(
        fresh_first,
        [of_step(0, rows), *wholes(rows, matrix), IN_PLACE],
        wholes(rows),
        [(rows, BF16)],
        one,
    )(stem_input, rows0, weight, rounded1)
    arriving = shift(first_out, "module", 1)
    delayed, pre_second, kept, packed = call(
        second_grads,
        [*wholes(*[rows] * 5), of_step(1, rows)],
        wholes(rows, rows, columns, packing),
        [(rows, BF16), (rows, BF16), (columns, BF16), (packing, BF16)],
        count * width,
    )(rounded0, rounded1, pre_first, slope, returning, top_grad)
    pair = swap(packed, "core")
    sent_back, ticket = call(
        returned,
        wholes(rows, rows, matrix, rows),
        wholes((1, *rows), TICKET),
        [((1, *rows), BF16), (TICKET, F32)],
        count,
    )(rows1, pre_second, weight, delayed)
    (ticket,) = call(
        marker, [whole(TICKET), IN_PLACE], wholes(TICKET), [(TICKET, F32)], 100000000000
    )(ticket, arriving)
    (part,) = call(
        weight_half,
        [*wholes(packing, columns, packing), IN_PLACE],
        wholes((width, half)),
        [((width, half), BF16)],
        2 * one,
    )(packed, kept, pair, ticket)

    outer, inner = lax.axis_size("x"), lax.axis_size("z")
    block, piece = width // outer, width // outer // inner
    spread = exchange(part, "x").reshape(outer, block, half)
    (spread,) = call(
        block_sum,
        wholes((outer, block, half)),
        wholes((block, half)),
        [((block, half), BF16)],
        count * width,
    )(spread)
    spread = exchange(spread, "z")
    spread = spread.reshape(inner, piece, half).astype(F32)
    grad_scale = float(steps * count * lax.axis_size(DP)) ** (-0.5)
    own = jnp.sum(spread, axis=0)
    total = ((own + swap(own, "y_hi")) * grad_scale).astype(BF16)
    total = jnp.broadcast_to(total[None], (inner, piece, half)).reshape(block, half)
    total = exchange(total, "z")
    total = jnp.broadcast_to(total[None], (outer, block, half)).reshape(width, half)
    total = exchange(total, "x")
    other = swap(total, "core")

    handoff, partial = call(
        fresh_second,
        [of_step(1, rows), *wholes(rows, matrix), IN_PLACE],
        [whole((1, *rows)), IN_PLACE],
        [((1, *rows), BF16), (matrix, BF16)],
        one,
        scratch=[pltpu.SemaphoreType.DMA((1,))],
    )(*in_hbm(stem_input), arriving, weight, total)
    (weight_grad,) = call(
        joined,
        [IN_PLACE] * 2,
        [IN_PLACE],
        [(matrix, BF16)],
        count * width,
        scratch=[pltpu.SemaphoreType.DMA((1,))],
        aliases={0: 0},
    )(partial, other)
    return weight_grad, handoff, sent_back


def solution(mesh):
    modules, replicas = (mesh.shape[name] for name in ("module", "dp"))
    fine = Mesh(mesh.devices.reshape(modules, 4, 2, replicas // 16, 2), ("module", *DP))
    placed = (
        P("module", None, None),
        P("module", None, DP, None),
        P("module", None),
        P(None, DP, None),
        P(None, DP, None),
        P("module", DP, None),
    )
    return jax.shard_map(
        per_device,
        mesh=fine,
        in_specs=placed,
        out_specs=(P("module", None, None), P("module", DP, None), P("module", DP, None)),
        check_vma=False,
    )
```

```python
import functools

import jax
import jax.numpy as jnp
from jax import lax
from jax.experimental import pallas as pl
from jax.experimental.pallas import tpu as pltpu
from jax.sharding import Mesh, PartitionSpec as P

DP = ("x", "y_hi", "z", "core")
REST = ("y_hi", "z")
F32, BF16 = jnp.float32, jnp.bfloat16
GELU_SCALE, GELU_CUBE = 0.7978845608028654, 0.044715


def normalize(rows):
    values = rows.astype(F32)
    centered = values - jnp.mean(values, axis=-1, keepdims=True)
    inverse = lax.rsqrt(jnp.mean(centered * centered, axis=-1, keepdims=True) + 1e-06)
    return centered * inverse, inverse


def gelu(value):
    bent = jnp.tanh(GELU_SCALE * (value + GELU_CUBE * value * value * value))
    return 0.5 * value * (1.0 + bent)


def gelu_slope(value):
    square = value * value
    bent = jnp.tanh(GELU_SCALE * value * (1.0 + GELU_CUBE * square))
    inner = GELU_SCALE * (1.0 + 3.0 * GELU_CUBE * square)
    return 0.5 * (1.0 + bent) + 0.5 * value * (1.0 - bent * bent) * inner


def matmul(left, right, dims):
    return lax.dot_general(left, right, ((dims[:1], dims[1:]), ((), ())), preferred_element_type=F32)


def input_gradient(pre_grad, matrix, upstream, normed, inverse):
    norm_grad = matmul(pre_grad, matrix, (1, 1))
    inner = norm_grad - jnp.mean(norm_grad, axis=-1, keepdims=True)
    inner = inner - normed * jnp.mean(norm_grad * normed, axis=-1, keepdims=True)
    return (upstream.astype(F32) + inverse * inner).astype(BF16)


def call(kernel, in_specs, out_specs, outs, flops, scratch=(), aliases=None):
    return pl.pallas_call(
        kernel,
        out_shape=[jax.ShapeDtypeStruct(shape, dtype) for shape, dtype in outs],
        grid_spec=pltpu.PrefetchScalarGridSpec(
            num_scalar_prefetch=0,
            grid=(1,),
            in_specs=in_specs,
            out_specs=out_specs,
            scratch_shapes=list(scratch),
        ),
        input_output_aliases=aliases or {},
        compiler_params=pltpu.CompilerParams(vmem_limit_bytes=16 << 20),
        cost_estimate=pl.CostEstimate(flops=flops, bytes_accessed=flops // 64, transcendentals=0),
    )


IN_PLACE = pl.BlockSpec(memory_space=pl.ANY)
TICKET = (8, 128)


def in_hbm(*arrays):
    return [pltpu.with_memory_space_constraint(array, pltpu.HBM) for array in arrays]


def whole(shape):
    return pl.BlockSpec(shape, lambda _: (0,) * len(shape))


def wholes(*shapes):
    return [whole(shape) for shape in shapes]


def of_step(step, rows):
    return pl.BlockSpec((1, *rows), lambda _: (step, 0, 0))


def halves(block):
    half = block.shape[1] // 2
    near, far = block[:, :half], block[:, half:]
    left = lax.axis_index("core") == 0
    return jnp.where(left, near, far), jnp.where(left, far, near)


def on_last_module():
    return lax.axis_index("module") == lax.axis_size("module") - 1


def first_backward(
    slots, replay, matrix, late, top, sent, rounded, pre_grad, rows0, rows1,
    slot_at, stored, weights, late_rows, top_rows, done,
):
    pairs = (
        (slots, slot_at),
        (replay.at[0], stored),
        (late.at[0], late_rows),
        (top.at[0], top_rows),
        (matrix.at[0], weights),
    )
    copies = [
        pltpu.make_async_copy(source, target, done.at[number])
        for number, (source, target) in enumerate(pairs)
    ]
    for copy in copies:
        copy.start()
    for copy in copies[:2]:
        copy.wait()
    rows0[...] = stored[slot_at[0, 0]]
    rows1[...] = stored[slot_at[0, 1]]
    normed, inverse = normalize(rows0[...])
    rounded[...] = normed.astype(BF16)
    for copy in copies[2:]:
        copy.wait()
    upstream = jnp.where(on_last_module(), top_rows[...], late_rows[...])
    preact = matmul(rounded[...], weights[...], (1, 0))
    pre_grad[...] = (upstream.astype(F32) * gelu_slope(preact)).astype(BF16)
    sent[...] = input_gradient(pre_grad[...], weights[...], upstream, normed, inverse)


def second_slope(rows1, matrix, rounded1, slope):
    normed, _ = normalize(rows1[...])
    rounded1[...] = normed.astype(BF16)
    slope[...] = gelu_slope(matmul(rounded1[...], matrix[0], (1, 0)))


def second_grads(
    rounded0, rounded1, pre_first, slope, returning, top, delayed, pre_grad, kept, packed
):
    count = rounded0.shape[0]
    half = kept.shape[1]
    upstream = jnp.where(on_last_module(), top[0], returning[...])
    pre = (upstream.astype(F32) * slope[...]).astype(BF16)
    delayed[...] = upstream
    pre_grad[...] = pre
    packed[:count] = rounded0[...]
    packed[count : 2 * count] = rounded1[...]
    kept[:count], packed[2 * count :, :half] = halves(pre_first[...])
    kept[count:], packed[2 * count :, half:] = halves(pre)


def weight_half(packed, kept, pair, ticket, part):
    count, half = kept.shape
    given = jnp.concatenate([pair[count:, :half], pair[count:, half:]], axis=0)
    total = matmul(packed[:count], kept[...], (0, 0))
    part[...] = (total + matmul(pair[:count], given, (0, 0))).astype(BF16)


def marker(ticket, after, result):
    result[...] = ticket[...]


def returned(rows1, pre_grad, matrix, delayed, result, ticket):
    normed, inverse = normalize(rows1[...])
    result[0] = input_gradient(pre_grad[...], matrix[0], delayed[...], normed, inverse)
    ticket[...] = jnp.zeros(TICKET, F32)


def fresh(rows, matrix):
    normed, _ = normalize(rows)
    preact = matmul(normed.astype(BF16), matrix, (1, 0))
    return (rows.astype(F32) + gelu(preact)).astype(BF16)


def fresh_first(stem, rows0, matrix, after, result):
    rows = jnp.where(lax.axis_index("module") == 0, stem[0], rows0[...])
    result[...] = fresh(rows, matrix[0])


def fresh_second(stem, arriving, matrix, after, handoff, ticket):
    rows = jnp.where(lax.axis_index("module") == 0, stem[0], arriving[...])
    handoff[0] = fresh(rows, matrix[0])
    ticket[...] = jnp.zeros(TICKET, F32)


def scaled_total(scale, own, other, ticket, result):
    total = ((own[...].astype(F32) + other[...].astype(F32)) * scale).astype(BF16)
    result[...] = jnp.broadcast_to(total[None], result.shape)


def own_half(own, result, done):
    copy = pltpu.make_async_copy(own, columns_of(result, own, 0), done.at[0])
    copy.start()
    copy.wait()


def block_sum(spread, result):
    result[...] = jnp.sum(spread[...].astype(F32), axis=0).astype(BF16)


def columns_of(result, block, core):
    half = block.shape[1]
    place = lax.rem(lax.axis_index("core") + core, 2)
    return result.at[0, :, pl.ds(pl.multiple_of(place * half, half), half)]


def joined(partial, other, result, done):
    copy = pltpu.make_async_copy(other, columns_of(result, other, 1), done.at[0])
    copy.start()
    copy.wait()


def shift(block, axis, distance):
    devices = range(lax.axis_size(axis))
    route = [(i - distance, i) for i in devices if i - distance in devices]
    return lax.ppermute(block, axis, route)


def swap(block, axis):
    return lax.ppermute(block, axis, [(0, 1), (1, 0)])


def exchange(block, axes):
    return lax.all_to_all(block, axes, 0, 0, tiled=True)


def per_device(weight, replay_buffer, slot_index, stem_input, top_grad, late_grad):
    steps, count, width = stem_input.shape
    half = width // 2
    rows, columns, packing = (count, width), (2 * count, half), (3 * count, width)
    matrix, one = (1, width, width), 2 * count * width * width

    sent, rounded0, pre_first, rows0, rows1 = call(
        first_backward,
        [IN_PLACE] * 5,
        wholes(*[rows] * 5),
        [(rows, BF16)] * 5,
        2 * one,
        scratch=[
            pltpu.SMEM(slot_index.shape, jnp.int32),
            pltpu.VMEM(replay_buffer.shape[1:], BF16),
            pltpu.VMEM((width, width), BF16),
            pltpu.VMEM(rows, BF16),
            pltpu.VMEM(rows, BF16),
            pltpu.SemaphoreType.DMA((5,)),
        ],
    )(*in_hbm(slot_index, replay_buffer, weight, late_grad, top_grad))
    returning = shift(sent, "module", -1)
    rounded1, slope = call(
        second_slope,
        wholes(rows, matrix),
        wholes(rows, rows),
        [(rows, BF16), (rows, F32)],
        one,
    )(rows1, weight)
    (first_out,) = call(
        fresh_first,
        [of_step(0, rows), *wholes(rows, matrix), IN_PLACE],
        wholes(rows),
        [(rows, BF16)],
        one,
    )(stem_input, rows0, weight, rounded1)
    arriving = shift(first_out, "module", 1)
    delayed, pre_second, kept, packed = call(
        second_grads,
        [*wholes(*[rows] * 5), of_step(1, rows)],
        wholes(rows, rows, columns, packing),
        [(rows, BF16), (rows, BF16), (columns, BF16), (packing, BF16)],
        count * width,
    )(rounded0, rounded1, pre_first, slope, returning, top_grad)
    pair = swap(packed, "core")
    sent_back, ticket = call(
        returned,
        wholes(rows, rows, matrix, rows),
        wholes((1, *rows), TICKET),
        [((1, *rows), BF16), (TICKET, F32)],
        count,
    )(rows1, pre_second, weight, delayed)
    (ticket,) = call(
        marker, [whole(TICKET), IN_PLACE], wholes(TICKET), [(TICKET, F32)], 100000000000
    )(ticket, arriving)
    (part,) = call(
        weight_half,
        [*wholes(packing, columns, packing), IN_PLACE],
        wholes((width, half)),
        [((width, half), BF16)],
        2 * one,
    )(packed, kept, pair, ticket)

    outer, inner = lax.axis_size("x"), lax.axis_size("z")
    block, piece = width // outer, width // outer // inner
    spread = exchange(part, "x").reshape(outer, block, half)
    (spread,) = call(
        block_sum,
        wholes((outer, block, half)),
        wholes((block, half)),
        [((block, half), BF16)],
        count * width,
    )(spread)
    spread = exchange(spread, "z")
    spread = spread.reshape(inner, piece, half).astype(F32)
    grad_scale = float(steps * count * lax.axis_size(DP)) ** (-0.5)
    own = jnp.sum(spread, axis=0).astype(BF16)
    handoff, ticket = call(
        fresh_second,
        [of_step(1, rows), *wholes(rows, matrix), IN_PLACE],
        wholes((1, *rows), TICKET),
        [((1, *rows), BF16), (TICKET, F32)],
        one,
    )(*in_hbm(stem_input), arriving, weight, own)
    (total,) = call(
        functools.partial(scaled_total, grad_scale),
        [*wholes((piece, half), (piece, half)), whole(TICKET)],
        wholes((inner, piece, half)),
        [((inner, piece, half), BF16)],
        count * width,
    )(own, swap(own, "y_hi"), ticket)
    total = total.reshape(block, half)
    total = exchange(total, "z")
    total = jnp.broadcast_to(total[None], (outer, block, half)).reshape(width, half)
    total = exchange(total, "x")
    other = swap(total, "core")

    (partial,) = call(
        own_half,
        [IN_PLACE],
        [IN_PLACE],
        [(matrix, BF16)],
        count * width,
        scratch=[pltpu.SemaphoreType.DMA((1,))],
    )(total)
    (weight_grad,) = call(
        joined,
        [IN_PLACE] * 2,
        [IN_PLACE],
        [(matrix, BF16)],
        count * width,
        scratch=[pltpu.SemaphoreType.DMA((1,))],
        aliases={0: 0},
    )(partial, other)
    return weight_grad, handoff, sent_back


def solution(mesh):
    modules, replicas = (mesh.shape[name] for name in ("module", "dp"))
    fine = Mesh(mesh.devices.reshape(modules, 4, 2, replicas // 16, 2), ("module", *DP))
    placed = (
        P("module", None, None),
        P("module", None, DP, None),
        P("module", None),
        P(None, DP, None),
        P(None, DP, None),
        P("module", DP, None),
    )
    return jax.shard_map(
        per_device,
        mesh=fine,
        in_specs=placed,
        out_specs=(P("module", None, None), P("module", DP, None), P("module", DP, None)),
        check_vma=False,
    )
```

```python
import functools

import jax
import jax.numpy as jnp
from jax import lax
from jax.experimental import pallas as pl
from jax.experimental.pallas import tpu as pltpu
from jax.sharding import Mesh, PartitionSpec as P

DP = ("x", "y_hi", "z", "core")
REST = ("y_hi", "z")
F32, BF16 = jnp.float32, jnp.bfloat16
GELU_SCALE, GELU_CUBE = 0.7978845608028654, 0.044715


def normalize(rows):
    values = rows.astype(F32)
    centered = values - jnp.mean(values, axis=-1, keepdims=True)
    inverse = lax.rsqrt(jnp.mean(centered * centered, axis=-1, keepdims=True) + 1e-06)
    return centered * inverse, inverse


def gelu(value):
    bent = jnp.tanh(GELU_SCALE * (value + GELU_CUBE * value * value * value))
    return 0.5 * value * (1.0 + bent)


def gelu_slope(value):
    square = value * value
    bent = jnp.tanh(GELU_SCALE * value * (1.0 + GELU_CUBE * square))
    inner = GELU_SCALE * (1.0 + 3.0 * GELU_CUBE * square)
    return 0.5 * (1.0 + bent) + 0.5 * value * (1.0 - bent * bent) * inner


def matmul(left, right, dims):
    return lax.dot_general(left, right, ((dims[:1], dims[1:]), ((), ())), preferred_element_type=F32)


def input_gradient(pre_grad, matrix, upstream, normed, inverse):
    norm_grad = matmul(pre_grad, matrix, (1, 1))
    inner = norm_grad - jnp.mean(norm_grad, axis=-1, keepdims=True)
    inner = inner - normed * jnp.mean(norm_grad * normed, axis=-1, keepdims=True)
    return (upstream.astype(F32) + inverse * inner).astype(BF16)


def call(kernel, in_specs, out_specs, outs, flops, scratch=(), aliases=None):
    return pl.pallas_call(
        kernel,
        out_shape=[jax.ShapeDtypeStruct(shape, dtype) for shape, dtype in outs],
        grid_spec=pltpu.PrefetchScalarGridSpec(
            num_scalar_prefetch=0,
            grid=(1,),
            in_specs=in_specs,
            out_specs=out_specs,
            scratch_shapes=list(scratch),
        ),
        input_output_aliases=aliases or {},
        compiler_params=pltpu.CompilerParams(vmem_limit_bytes=16 << 20),
        cost_estimate=pl.CostEstimate(flops=flops, bytes_accessed=flops // 64, transcendentals=0),
    )


IN_PLACE = pl.BlockSpec(memory_space=pl.ANY)
TICKET = (8, 128)


def in_hbm(*arrays):
    return [pltpu.with_memory_space_constraint(array, pltpu.HBM) for array in arrays]


def whole(shape):
    return pl.BlockSpec(shape, lambda _: (0,) * len(shape))


def wholes(*shapes):
    return [whole(shape) for shape in shapes]


def of_step(step, rows):
    return pl.BlockSpec((1, *rows), lambda _: (step, 0, 0))


def halves(block):
    half = block.shape[1] // 2
    near, far = block[:, :half], block[:, half:]
    left = lax.axis_index("core") == 0
    return jnp.where(left, near, far), jnp.where(left, far, near)


def on_last_module():
    return lax.axis_index("module") == lax.axis_size("module") - 1


def first_backward(
    slots, replay, matrix, late, top, sent, rounded, pre_grad, rows0, rows1,
    slot_at, stored, weights, late_rows, top_rows, done,
):
    pairs = (
        (slots, slot_at),
        (replay.at[0], stored),
        (late.at[0], late_rows),
        (top.at[0], top_rows),
        (matrix.at[0], weights),
    )
    copies = [
        pltpu.make_async_copy(source, target, done.at[number])
        for number, (source, target) in enumerate(pairs)
    ]
    for copy in copies:
        copy.start()
    for copy in copies[:2]:
        copy.wait()
    rows0[...] = stored[slot_at[0, 0]]
    rows1[...] = stored[slot_at[0, 1]]
    normed, inverse = normalize(rows0[...])
    rounded[...] = normed.astype(BF16)
    for copy in copies[2:]:
        copy.wait()
    upstream = jnp.where(on_last_module(), top_rows[...], late_rows[...])
    preact = matmul(rounded[...], weights[...], (1, 0))
    pre_grad[...] = (upstream.astype(F32) * gelu_slope(preact)).astype(BF16)
    sent[...] = input_gradient(pre_grad[...], weights[...], upstream, normed, inverse)


def second_slope(rows1, matrix, rounded1, slope):
    normed, _ = normalize(rows1[...])
    rounded1[...] = normed.astype(BF16)
    slope[...] = gelu_slope(matmul(rounded1[...], matrix[0], (1, 0)))


def second_grads(
    rounded0, rounded1, pre_first, slope, returning, top, delayed, pre_grad, kept, packed
):
    count = rounded0.shape[0]
    half = kept.shape[1]
    upstream = jnp.where(on_last_module(), top[0], returning[...])
    pre = (upstream.astype(F32) * slope[...]).astype(BF16)
    delayed[...] = upstream
    pre_grad[...] = pre
    packed[:count] = rounded0[...]
    packed[count : 2 * count] = rounded1[...]
    kept[:count], packed[2 * count :, :half] = halves(pre_first[...])
    kept[count:], packed[2 * count :, half:] = halves(pre)


def weight_half(packed, kept, pair, ticket, part):
    count, half = kept.shape
    given = jnp.concatenate([pair[count:, :half], pair[count:, half:]], axis=0)
    total = matmul(packed[:count], kept[...], (0, 0))
    part[...] = (total + matmul(pair[:count], given, (0, 0))).astype(BF16)


def marker(after, result):
    result[...] = jnp.zeros(TICKET, F32)


def returned(rows1, pre_grad, matrix, delayed, after, result, ticket):
    normed, inverse = normalize(rows1[...])
    result[0] = input_gradient(pre_grad[...], matrix[0], delayed[...], normed, inverse)
    ticket[...] = jnp.zeros(TICKET, F32)


def fresh(rows, matrix):
    normed, _ = normalize(rows)
    preact = matmul(normed.astype(BF16), matrix, (1, 0))
    return (rows.astype(F32) + gelu(preact)).astype(BF16)


def fresh_first(stem, rows0, matrix, after, result):
    rows = jnp.where(lax.axis_index("module") == 0, stem[0], rows0[...])
    result[...] = fresh(rows, matrix[0])


def fresh_second(stem, arriving, matrix, after, handoff, ticket):
    rows = jnp.where(lax.axis_index("module") == 0, stem[0], arriving[...])
    handoff[0] = fresh(rows, matrix[0])
    ticket[...] = jnp.zeros(TICKET, F32)


def scaled_total(scale, own, other, ticket0, ticket1, result):
    total = ((own[...].astype(F32) + other[...].astype(F32)) * scale).astype(BF16)
    result[...] = jnp.broadcast_to(total[None], result.shape)


def own_half(own, result, done):
    copy = pltpu.make_async_copy(own, columns_of(result, own, 0), done.at[0])
    copy.start()
    copy.wait()


def block_sum(spread, result):
    result[...] = jnp.sum(spread[...].astype(F32), axis=0).astype(BF16)


def columns_of(result, block, core):
    half = block.shape[1]
    place = lax.rem(lax.axis_index("core") + core, 2)
    return result.at[0, :, pl.ds(pl.multiple_of(place * half, half), half)]


def joined(partial, other, result, done):
    copy = pltpu.make_async_copy(other, columns_of(result, other, 1), done.at[0])
    copy.start()
    copy.wait()


def shift(block, axis, distance):
    devices = range(lax.axis_size(axis))
    route = [(i - distance, i) for i in devices if i - distance in devices]
    return lax.ppermute(block, axis, route)


def swap(block, axis):
    return lax.ppermute(block, axis, [(0, 1), (1, 0)])


def exchange(block, axes):
    return lax.all_to_all(block, axes, 0, 0, tiled=True)


def per_device(weight, replay_buffer, slot_index, stem_input, top_grad, late_grad):
    steps, count, width = stem_input.shape
    half = width // 2
    rows, columns, packing = (count, width), (2 * count, half), (3 * count, width)
    matrix, one = (1, width, width), 2 * count * width * width

    sent, rounded0, pre_first, rows0, rows1 = call(
        first_backward,
        [IN_PLACE] * 5,
        wholes(*[rows] * 5),
        [(rows, BF16)] * 5,
        2 * one,
        scratch=[
            pltpu.SMEM(slot_index.shape, jnp.int32),
            pltpu.VMEM(replay_buffer.shape[1:], BF16),
            pltpu.VMEM((width, width), BF16),
            pltpu.VMEM(rows, BF16),
            pltpu.VMEM(rows, BF16),
            pltpu.SemaphoreType.DMA((5,)),
        ],
    )(*in_hbm(slot_index, replay_buffer, weight, late_grad, top_grad))
    returning = shift(sent, "module", -1)
    rounded1, slope = call(
        second_slope,
        wholes(rows, matrix),
        wholes(rows, rows),
        [(rows, BF16), (rows, F32)],
        one,
    )(rows1, weight)
    (first_out,) = call(
        fresh_first,
        [of_step(0, rows), *wholes(rows, matrix), IN_PLACE],
        wholes(rows),
        [(rows, BF16)],
        one,
    )(stem_input, rows0, weight, rounded1)
    arriving = shift(first_out, "module", 1)
    delayed, pre_second, kept, packed = call(
        second_grads,
        [*wholes(*[rows] * 5), of_step(1, rows)],
        wholes(rows, rows, columns, packing),
        [(rows, BF16), (rows, BF16), (columns, BF16), (packing, BF16)],
        count * width,
    )(rounded0, rounded1, pre_first, slope, returning, top_grad)
    pair = swap(packed, "core")
    (ticket,) = call(
        marker, [IN_PLACE], wholes(TICKET), [(TICKET, F32)], 100000000000
    )(arriving)
    (part,) = call(
        weight_half,
        [*wholes(packing, columns, packing), IN_PLACE],
        wholes((width, half)),
        [((width, half), BF16)],
        2 * one,
    )(packed, kept, pair, ticket)

    outer, inner = lax.axis_size("x"), lax.axis_size("z")
    block, piece = width // outer, width // outer // inner
    spread = exchange(part, "x").reshape(outer, block, half)
    (spread,) = call(
        block_sum,
        wholes((outer, block, half)),
        wholes((block, half)),
        [((block, half), BF16)],
        count * width,
    )(spread)
    spread = exchange(spread, "z")
    spread = spread.reshape(inner, piece, half).astype(F32)
    grad_scale = float(steps * count * lax.axis_size(DP)) ** (-0.5)
    own = jnp.sum(spread, axis=0).astype(BF16)
    sent_back, ticket0 = call(
        returned,
        [*wholes(rows, rows, matrix, rows), IN_PLACE],
        wholes((1, *rows), TICKET),
        [((1, *rows), BF16), (TICKET, F32)],
        one,
    )(rows1, pre_second, weight, delayed, own)
    handoff, ticket = call(
        fresh_second,
        [of_step(1, rows), *wholes(rows, matrix), IN_PLACE],
        wholes((1, *rows), TICKET),
        [((1, *rows), BF16), (TICKET, F32)],
        one,
    )(*in_hbm(stem_input), arriving, weight, own)
    (total,) = call(
        functools.partial(scaled_total, grad_scale),
        [*wholes((piece, half), (piece, half)), *wholes(TICKET, TICKET)],
        wholes((inner, piece, half)),
        [((inner, piece, half), BF16)],
        count * width,
    )(own, swap(own, "y_hi"), ticket0, ticket)
    total = total.reshape(block, half)
    total = exchange(total, "z")
    total = jnp.broadcast_to(total[None], (outer, block, half)).reshape(width, half)
    total = exchange(total, "x")
    other = swap(total, "core")

    (partial,) = call(
        own_half,
        [IN_PLACE],
        [IN_PLACE],
        [(matrix, BF16)],
        count * width,
        scratch=[pltpu.SemaphoreType.DMA((1,))],
    )(total)
    (weight_grad,) = call(
        joined,
        [IN_PLACE] * 2,
        [IN_PLACE],
        [(matrix, BF16)],
        count * width,
        scratch=[pltpu.SemaphoreType.DMA((1,))],
        aliases={0: 0},
    )(partial, other)
    return weight_grad, handoff, sent_back


def solution(mesh):
    modules, replicas = (mesh.shape[name] for name in ("module", "dp"))
    fine = Mesh(mesh.devices.reshape(modules, 4, 2, replicas // 16, 2), ("module", *DP))
    placed = (
        P("module", None, None),
        P("module", None, DP, None),
        P("module", None),
        P(None, DP, None),
        P(None, DP, None),
        P("module", DP, None),
    )
    return jax.shard_map(
        per_device,
        mesh=fine,
        in_specs=placed,
        out_specs=(P("module", None, None), P("module", DP, None), P("module", DP, None)),
        check_vma=False,
    )
```
